32 devices in a mesh: fsdp: 4 (over z), expert: 8 (over y, x, core).
Axes of the slice: x: 2, y: 2, z: 4, core: 2. Of those that a mesh axis runs over, the one named last changes fastest.
Arguments:
- tokens: bfloat16 [512, 6144], P('expert', 'fsdp'), may hold values from -6 to 6
- expert_ids: int32 [512, 2], P('expert'), may hold values from 0 to 7, all different within a row; in each aligned block of 64 rows (0 to 63, 64 to 127, ...) at most 24 rows name the same one
- gate_values: float32 [512, 2], P('expert'), may hold values from 0.1 to 1
- w_gate: bfloat16 [6144, 65536], P('fsdp', 'expert'), may hold values from -0.078125 to 0.078125
- w_up: bfloat16 [6144, 65536], P('fsdp', 'expert'), may hold values from -0.078125 to 0.078125
- w_down: bfloat16 [65536, 6144], P('expert', 'fsdp'), may hold values from -0.0625 to 0.0625
- scale_gate: float32 [48, 512], P('fsdp', 'expert'), may hold values from 0.5 to 2
- scale_up: float32 [48, 512], P('fsdp', 'expert'), may hold values from 0.5 to 2
- scale_down: float32 [512, 48], P('expert', 'fsdp'), may hold values from 0.5 to 2
Outputs:
- mixed: bfloat16 [512, 6144], P('expert', 'fsdp')
The draws below stay inside these ranges and needn't reach their ends.
Inputs may be any that keep to these rules, and one draw needn't show every extreme that they name: `expert_ids`: within the 64 rows of each index of expert (aligned blocks of rows), no expert id occurs in more than 24 rows, and some id occurs in exactly 24 rows of some block; the two ids of a row differ; every id occurs somewhere.
All inputs are finite; a program needn't handle non-finite values.
Results may differ from the reference program's by a relative error of at most 0.03.
Values may be sent and summed in bfloat16 or wider, within the bound.
No kernel may reach another device: no remote copies, remote signals or barrier semaphores. Data moves between devices by JAX's collectives and lax.ppermute only.
A program may use at most 192 MiB of HBM per device.

```python
import math
import jax
import jax.numpy as jnp
import numpy as np
from jax import lax

D = 6144
EXPERTS = 8
HIDDEN_SIZE = 8192
BLOCK = 128
TOK = 64
CAP = 24
TOKENS = 512
N_FSDP = 4
N_EXPERT = 8


def shard_levels(rng, extent, split, low, largest):
    def one(dim, parts):
        steps = jax.random.uniform(jax.random.fold_in(jax.random.fold_in(rng, 6), dim), (parts,), jnp.float32, low / len(split), largest / len(split))
        return jnp.repeat(jnp.exp(steps), extent[dim] // parts).reshape((-1,) + (1,) * (len(extent) - dim - 1))

    gain = one(*split[0])
    for cut in split[1:]:
        gain = gain * one(*cut)
    return gain


def routed_block(stream_key, own, number, rows, count, top, bound, lean):
    order = jax.random.permutation(stream_key, count)
    crowded, ordinary = load_shares(count, rows * top, bound, lean, True), load_shares(count, rows * top, bound, lean, False)
    places = jnp.arange(count)

    def named(sizes, turn):
        used = int((sizes > 0).sum())
        fixed = max(1, used // 4)
        shifted = fixed + (places - fixed + turn * (used - fixed)) % max(1, count - fixed)
        return jnp.zeros((count,), jnp.int32).at[order[jnp.where(places < fixed, places, shifted)]].set(jnp.asarray(sizes, jnp.int32))

    sizes = jnp.where(number % 4 == 0, named(crowded, number // 4), named(ordinary, number - number // 4 - 1))
    mixed = jax.random.permutation(jax.random.fold_in(own, 3), count)
    source_of, receiver = mixed[0:count // 2 * 2:2], mixed[1:count // 2 * 2:2]
    margin = jnp.minimum(sizes[source_of] - 1, bound - sizes[receiver]) // 2
    margin = jnp.where((source_of == order[0]) | (receiver == order[0]) | (sizes[receiver] == 0), 0, jnp.maximum(margin, 0))
    shifted = jax.random.randint(jax.random.fold_in(own, 4), (count // 2,), 0, 1 << 20) % (margin + 1)
    sizes = sizes.at[source_of].add(-shifted).at[receiver].add(shifted)
    members = jnp.searchsorted(jnp.cumsum(sizes), jnp.arange(rows * top), side="right").astype(jnp.int32)
    table = members.reshape(top, rows).T
    table = table[jax.random.permutation(jax.random.fold_in(own, 1), rows)]
    turn = jax.random.randint(jax.random.fold_in(own, 2), (rows, 1), 0, top)
    return jnp.take_along_axis(table, (jnp.arange(top)[None, :] + turn) % top, axis=1)


def load_shares(number_of, total, bound, lean, full):
    weights = [(1 << 20) // math.isqrt(standing ** lean) + 1 for standing in range(1, number_of + 1)]
    largest = bound if full else min(bound, max(-(-total // number_of), total * weights[0] // sum(weights)))
    least = 1 if total - largest >= number_of - 1 else 0
    holding, rest = [largest] + [least] * (number_of - 1), total - largest - least * (number_of - 1)
    while rest > 0:
        free = [i for i in range(1, number_of) if holding[i] < largest] or [i for i in range(1, number_of) if holding[i] < bound]
        pool, left = sum([weights[i] for i in free]), rest
        for i in free:
            extra = min(bound - holding[i], max(1, left * weights[i] // pool), rest)
            holding[i] = holding[i] + extra
            rest = rest - extra
    return np.array(holding)


def bell_draw(key, dims, deviation, most, cuts=(), kind=jnp.bfloat16):
    factor_of = shard_levels(key, dims, cuts, -0.22, 0.18) if cuts else 1.0
    values = jax.random.normal(key, dims, jnp.float32) * deviation * factor_of
    return jnp.minimum(jnp.maximum(values, -most), most).astype(kind)


def setup_inputs(seed: int = 0) -> dict:
    arg_keys = jax.random.split(jax.random.key(seed), 10)
    tokens = bell_draw(arg_keys[0], (TOKENS, D), 1.0, 6.0, ((0, 8), (1, 4)))
    expert_ids_keys = jax.random.split(jax.random.fold_in(arg_keys[1], 1), TOKENS // TOK)
    expert_ids_turns = jax.random.permutation(jax.random.fold_in(arg_keys[1], 3), TOKENS // TOK)
    expert_ids = jax.vmap(lambda own, number: routed_block(jax.random.fold_in(arg_keys[1], 2), own, number, TOK, EXPERTS, 2, CAP, 2))(expert_ids_keys, expert_ids_turns).reshape((TOKENS, 2))
    gate_values = jnp.clip(0.1 + 0.9 * jax.random.uniform(arg_keys[2], (TOKENS, 2), jnp.float32) ** shard_levels(arg_keys[2], (TOKENS, 2), ((0, 8),), -0.2, 0.2), 0.1, 1.0)
    w_gate = bell_draw(arg_keys[3], (D, EXPERTS * HIDDEN_SIZE), D ** -0.5, 0.078125, ((0, 4), (1, 8)))
    w_up = bell_draw(arg_keys[4], (D, EXPERTS * HIDDEN_SIZE), D ** -0.5, 0.078125, ((0, 4), (1, 8)))
    w_down = bell_draw(arg_keys[5], (EXPERTS * HIDDEN_SIZE, D), HIDDEN_SIZE ** -0.5, 0.0625, ((0, 8), (1, 4)))
    scale_gate = jnp.clip(jnp.exp(math.log(2.0) - 1.3862944 * jax.random.uniform(arg_keys[6], (D // BLOCK, EXPERTS * HIDDEN_SIZE // BLOCK), jnp.float32) ** shard_levels(arg_keys[6], (D // BLOCK, EXPERTS * HIDDEN_SIZE // BLOCK), ((0, 4), (1, 8)), -0.2, 0.2)), 0.5, 2.0)
    scale_up = jnp.clip(jnp.exp(math.log(2.0) - 1.3862944 * jax.random.uniform(arg_keys[7], (D // BLOCK, EXPERTS * HIDDEN_SIZE // BLOCK), jnp.float32) ** shard_levels(arg_keys[7], (D // BLOCK, EXPERTS * HIDDEN_SIZE // BLOCK), ((0, 4), (1, 8)), -0.2, 0.2)), 0.5, 2.0)
    scale_down = jnp.clip(jnp.exp(math.log(2.0) - 1.3862944 * jax.random.uniform(arg_keys[8], (EXPERTS * HIDDEN_SIZE // BLOCK, D // BLOCK), jnp.float32) ** shard_levels(arg_keys[8], (EXPERTS * HIDDEN_SIZE // BLOCK, D // BLOCK), ((0, 8), (1, 4)), -0.2, 0.2)), 0.5, 2.0)
    return dict(tokens=tokens, expert_ids=expert_ids, gate_values=gate_values, w_gate=w_gate, w_up=w_up, w_down=w_down, scale_gate=scale_gate, scale_up=scale_up, scale_down=scale_down)


def rounded(values):
    return lax.optimization_barrier(values.astype(jnp.bfloat16)).astype(jnp.float32)


def dequant(weights, block_scale):
    spread = jnp.repeat(jnp.repeat(block_scale, BLOCK, axis=0), BLOCK, axis=1)
    return (weights.astype(jnp.float32) * spread.astype(jnp.float32)).astype(jnp.bfloat16)


def reference(tokens, expert_ids, gate_values, w_gate, w_up, w_down, scale_gate, scale_up, scale_down):
    slices = N_EXPERT // EXPERTS
    feature_width = D // N_FSDP
    slice_width = HIDDEN_SIZE // slices
    buffer_rows = N_EXPERT * CAP
    scale_cols = HIDDEN_SIZE // BLOCK
    flat_ids = expert_ids.reshape(-1).astype(jnp.int32)
    owners = jnp.repeat(jnp.arange(TOKENS, dtype=jnp.int32), 2)
    onehot = (flat_ids[:, None] == jnp.arange(EXPERTS, dtype=jnp.int32)[None, :]).astype(jnp.int32)
    slot_rank = jnp.sum((jnp.cumsum(onehot, axis=0) - onehot) * onehot, axis=1).astype(jnp.int32)
    buffers = jnp.zeros((EXPERTS, buffer_rows, D), jnp.bfloat16).at[flat_ids, slot_rank].set(tokens[owners])

    def expert_out(expert_index):
        rows_in = buffers[expert_index]
        col_start = expert_index * HIDDEN_SIZE
        scale_start = expert_index * scale_cols
        gate_deq = dequant(lax.dynamic_slice_in_dim(w_gate, col_start, HIDDEN_SIZE, 1),
                           lax.dynamic_slice_in_dim(scale_gate, scale_start, scale_cols, 1))
        up_deq = dequant(lax.dynamic_slice_in_dim(w_up, col_start, HIDDEN_SIZE, 1),
                         lax.dynamic_slice_in_dim(scale_up, scale_start, scale_cols, 1))
        down_deq = dequant(lax.dynamic_slice_in_dim(w_down, col_start, HIDDEN_SIZE, 0),
                           lax.dynamic_slice_in_dim(scale_down, scale_start, scale_cols, 0))
        gate_sum = jnp.zeros((buffer_rows, HIDDEN_SIZE), jnp.float32)
        up_sum = jnp.zeros((buffer_rows, HIDDEN_SIZE), jnp.float32)
        for block_index in range(N_FSDP):
            low_edge = block_index * feature_width
            high_edge = low_edge + feature_width
            gate_sum = gate_sum + rounded(jnp.dot(rows_in[:, low_edge:high_edge], gate_deq[low_edge:high_edge], preferred_element_type=jnp.float32))
            up_sum = up_sum + rounded(jnp.dot(rows_in[:, low_edge:high_edge], up_deq[low_edge:high_edge], preferred_element_type=jnp.float32))
        hidden = (jax.nn.silu(gate_sum) * up_sum).astype(jnp.bfloat16)
        output = jnp.zeros((buffer_rows, D), jnp.float32)
        for slice_index in range(slices):
            low_edge = slice_index * slice_width
            high_edge = low_edge + slice_width
            output = output + rounded(jnp.dot(hidden[:, low_edge:high_edge], down_deq[low_edge:high_edge], preferred_element_type=jnp.float32))
        return output

    per_expert = lax.map(expert_out, jnp.arange(EXPERTS, dtype=jnp.int32))
    per_assign = per_expert[flat_ids, slot_rank]
    weighted = per_assign * gate_values.reshape(-1)[:, None].astype(jnp.float32)
    return jnp.sum(weighted.reshape(TOKENS, 2, D), axis=1).astype(jnp.bfloat16)
```

```python
import functools

import jax
import jax.numpy as jnp
from jax import lax
from jax.experimental import pallas as pl
from jax.experimental.pallas import tpu as pltpu
from jax.sharding import PartitionSpec as P

EXPERTS = 8
BLOCK = 128
CAP = 24
CHUNKS = 4


def widen(block_scale):
    return jnp.repeat(block_scale, BLOCK, axis=1).astype(jnp.bfloat16)


def spread(weights, scale_rows):
    depth, width = weights.shape
    parts = [
        weights[k * BLOCK : (k + 1) * BLOCK, :] * scale_rows[k : k + 1, :]
        for k in range(depth // BLOCK)
    ]
    return jnp.concatenate(parts, axis=0) if len(parts) > 1 else parts[0]


def own_kernel(index_ref, x_ref, gate_ref, up_ref, gate_scale_ref, up_scale_ref, out_ref):
    x = x_ref[...]
    out_ref[0] = jnp.dot(
        x, spread(gate_ref[...], gate_scale_ref[...]), preferred_element_type=jnp.float32
    ).astype(jnp.bfloat16)
    out_ref[1] = jnp.dot(
        x, spread(up_ref[...], up_scale_ref[...]), preferred_element_type=jnp.float32
    ).astype(jnp.bfloat16)


def own_terms(index, x, w_gate, w_up, gate_scale, up_scale, chunk):
    rows, depth = x.shape
    width = min(256, chunk)
    steps = chunk // width
    column = lambda j, index: (0, index[0] * steps + j)
    weight_spec = pl.BlockSpec((depth, width), column)
    scale_spec = pl.BlockSpec((depth // BLOCK, width), column)
    return pl.pallas_call(
        own_kernel,
        grid_spec=pltpu.PrefetchScalarGridSpec(
            num_scalar_prefetch=1,
            grid=(steps,),
            in_specs=[
                pl.BlockSpec((rows, depth), lambda j, index: (0, 0)),
                weight_spec,
                weight_spec,
                scale_spec,
                scale_spec,
            ],
            out_specs=pl.BlockSpec((2, rows, width), lambda j, index: (0, 0, j)),
        ),
        out_shape=jax.ShapeDtypeStruct((2, rows, chunk), jnp.bfloat16),
        compiler_params=pltpu.CompilerParams(vmem_limit_bytes=32 * 1024 * 1024),
        cost_estimate=pl.CostEstimate(
            flops=4 * rows * depth * chunk, bytes_accessed=4 * depth * chunk, transcendentals=0
        ),
        name="gate_up",
    )(index, x, w_gate, w_up, gate_scale, up_scale)


def down_kernel(index_ref, hidden_ref, weight_ref, scale_ref, total_ref, out_ref):
    step = pl.program_id(0)

    @pl.when(step == 0)
    def _():
        out_ref[...] = total_ref[...]

    @pl.when(index_ref[1] > 0)
    def _():
        out_ref[...] += jnp.dot(
            hidden_ref[...],
            spread(weight_ref[...], scale_ref[0]),
            preferred_element_type=jnp.float32,
        )


def down_add(index, hidden, w_down, down_scale, total):
    rows, chunk = hidden.shape
    width = w_down.shape[1]
    depth = min(256, chunk)
    steps = chunk // depth
    at = lambda j, index: index[0] * steps + jnp.where(index[1] > 0, j, 0)
    scale = down_scale.reshape(-1, depth // BLOCK, width)
    return pl.pallas_call(
        down_kernel,
        grid_spec=pltpu.PrefetchScalarGridSpec(
            num_scalar_prefetch=1,
            grid=(steps,),
            in_specs=[
                pl.BlockSpec((rows, depth), lambda j, index: (0, j)),
                pl.BlockSpec((depth, width), lambda j, index: (at(j, index), 0)),
                pl.BlockSpec((1, depth // BLOCK, width), lambda j, index: (at(j, index), 0, 0)),
                pl.BlockSpec((rows, width), lambda j, index: (0, 0)),
            ],
            out_specs=pl.BlockSpec((rows, width), lambda j, index: (0, 0)),
        ),
        out_shape=jax.ShapeDtypeStruct((rows, width), jnp.float32),
        input_output_aliases={4: 0},
        compiler_params=pltpu.CompilerParams(vmem_limit_bytes=32 * 1024 * 1024),
        cost_estimate=pl.CostEstimate(
            flops=2 * rows * width * chunk, bytes_accessed=2 * width * chunk, transcendentals=0
        ),
        name="down",
    )(index, hidden, w_down, scale, total)


def activate(gate, up):
    gate, up = gate.astype(jnp.float32), up.astype(jnp.float32)
    return (jax.nn.silu(gate) * up).astype(jnp.bfloat16)


def expert_rows(x, w_gate, w_up, w_down, gate_scale, up_scale, down_scale):
    hidden_width = w_gate.shape[1]
    chunk = hidden_width // CHUNKS
    total = jnp.zeros((x.shape[0], w_down.shape[1]), jnp.float32)
    sums = []
    for c in range(CHUNKS):
        own = own_terms(jnp.array([c], jnp.int32), x, w_gate, w_up, gate_scale, up_scale, chunk)
        sums.append(lax.psum_scatter(own, "fsdp", scatter_dimension=1, tiled=True))
    for c in range(CHUNKS):
        hidden = lax.all_gather(activate(sums[c][0], sums[c][1]), "fsdp", axis=0, tiled=True)
        total = down_add(jnp.array([c, 1], jnp.int32), hidden, w_down, down_scale, total)
    return total


def shards(tokens, expert_ids, gate_values, w_gate, w_up, w_down, scale_gate, scale_up, scale_down):
    device_count = lax.axis_size("expert")
    slices = device_count // EXPERTS
    local_tokens = tokens.shape[0]
    feature_cols = tokens.shape[1]
    slot_total = EXPERTS * CAP
    flat_ids = expert_ids.reshape(-1)
    onehot = (flat_ids[:, None] == jnp.arange(EXPERTS, dtype=jnp.int32)[None, :]).astype(jnp.int32)
    slot_rank = jnp.sum((jnp.cumsum(onehot, axis=0) - onehot) * onehot, axis=1)
    target = flat_ids * CAP + slot_rank
    placing = (target[:, None] == jnp.arange(slot_total, dtype=jnp.int32)[None, :]).astype(
        jnp.float32
    )
    token_map = jnp.sum(placing.reshape(local_tokens, 2, slot_total), axis=1).astype(jnp.bfloat16)
    packed = jnp.einsum("ts,td->sd", token_map, tokens, preferred_element_type=jnp.float32).astype(
        jnp.bfloat16
    )
    outgoing = jnp.broadcast_to(
        packed.reshape(EXPERTS, 1, CAP, feature_cols), (EXPERTS, slices, CAP, feature_cols)
    ).reshape(device_count * CAP, feature_cols)
    incoming = lax.all_to_all(outgoing, "expert", split_axis=0, concat_axis=0, tiled=True)
    partial_rows = expert_rows(
        incoming, w_gate, w_up, w_down, widen(scale_gate), widen(scale_up), widen(scale_down)
    ).astype(jnp.bfloat16)
    returned = lax.all_to_all(partial_rows, "expert", split_axis=0, concat_axis=0, tiled=True)
    slice_sums = jnp.sum(
        returned.reshape(EXPERTS, slices, CAP, feature_cols).astype(jnp.float32), axis=1
    )
    slice_sums = slice_sums.reshape(slot_total, feature_cols)
    weights_map = jnp.sum(
        (placing * gate_values.reshape(-1)[:, None]).reshape(local_tokens, 2, slot_total), axis=1
    )
    mixed_rows = jnp.dot(
        weights_map, slice_sums, precision=lax.Precision.HIGHEST, preferred_element_type=jnp.float32
    )
    return mixed_rows.astype(jnp.bfloat16)


def solution(mesh):
    in_specs = (
        P("expert", "fsdp"),
        P("expert", None),
        P("expert", None),
        P("fsdp", "expert"),
        P("fsdp", "expert"),
        P("expert", "fsdp"),
        P("fsdp", "expert"),
        P("fsdp", "expert"),
        P("expert", "fsdp"),
    )
    out_specs = P("expert", "fsdp")
    return jax.shard_map(shards, mesh=mesh, in_specs=in_specs, out_specs=out_specs, check_vma=False)
```

```python
import functools

import jax
import jax.numpy as jnp
from jax import lax
from jax.experimental import pallas as pl
from jax.experimental.pallas import tpu as pltpu
from jax.sharding import PartitionSpec as P

EXPERTS = 8
BLOCK = 128
CAP = 24
UNITS = 8
CHAIN_UNITS = 8
LAG = 2
GROUP = 1


def widen(block_scale):
    return jnp.repeat(block_scale, BLOCK, axis=1).astype(jnp.bfloat16)


def spread(weights, scale_rows):
    depth = weights.shape[0]
    parts = [
        weights[k * BLOCK : (k + 1) * BLOCK, :] * scale_rows[k : k + 1, :]
        for k in range(depth // BLOCK)
    ]
    return jnp.concatenate(parts, axis=0) if len(parts) > 1 else parts[0]


def own_kernel(index_ref, x_ref, gate_ref, up_ref, gate_scale_ref, up_scale_ref, out_ref):
    @pl.when(index_ref[1] > 0)
    def _():
        x = x_ref[...]
        out_ref[0] = jnp.dot(
            x, spread(gate_ref[...], gate_scale_ref[...]), preferred_element_type=jnp.float32
        ).astype(jnp.bfloat16)
        out_ref[1] = jnp.dot(
            x, spread(up_ref[...], up_scale_ref[...]), preferred_element_type=jnp.float32
        ).astype(jnp.bfloat16)


def tile(width, most):
    return max(t for t in range(BLOCK, most + 1, BLOCK) if width % t == 0)


def own_terms(index, x, weights, count):
    w_gate, w_up, gate_scale, up_scale = weights
    rows, depth = x.shape
    width = own_tile(count)
    column = lambda j, index: (0, index[0] + jnp.where(index[1] > 0, j, 0))
    weight_spec = pl.BlockSpec((depth, width), column)
    scale_spec = pl.BlockSpec((depth // BLOCK, width), column)
    return pl.pallas_call(
        own_kernel,
        grid_spec=pltpu.PrefetchScalarGridSpec(
            num_scalar_prefetch=1,
            grid=(count // width,),
            in_specs=[
                pl.BlockSpec((rows, depth), lambda j, index: (0, 0)),
                weight_spec,
                weight_spec,
                scale_spec,
                scale_spec,
            ],
            out_specs=pl.BlockSpec((2, rows, width), lambda j, index: (0, 0, j)),
        ),
        out_shape=jax.ShapeDtypeStruct((2, rows, count), jnp.bfloat16),
        compiler_params=pltpu.CompilerParams(vmem_limit_bytes=32 * 1024 * 1024),
        cost_estimate=pl.CostEstimate(
            flops=4 * rows * depth * count, bytes_accessed=8 * depth * count, transcendentals=0
        ),
        name="gate_up",
    )(index, x, w_gate, w_up, gate_scale, up_scale)


def own_tile(count):
    return tile(count, 512)


def down_kernel(index_ref, hidden_ref, weight_ref, scale_ref, total_ref, out_ref, *, steps):
    step = pl.program_id(0)

    @pl.when(step == 0)
    def _():
        out_ref[...] = total_ref[...]

    @pl.when(index_ref[1, step // steps] > 0)
    def _():
        out_ref[...] += jnp.dot(
            hidden_ref[0],
            spread(weight_ref[...], scale_ref[0]),
            preferred_element_type=jnp.float32,
        )


def down_add(index, hidden, w_down, down_scale, total):
    count, rows, unit = hidden.shape
    width = w_down.shape[1]
    depth = tile(unit, 512)
    steps = unit // depth

    def at(j, index):
        slot = j // steps
        return index[0, slot] * steps + jnp.where(index[1, slot] > 0, j % steps, 0)

    scale = down_scale.reshape(-1, depth // BLOCK, width)
    return pl.pallas_call(
        functools.partial(down_kernel, steps=steps),
        grid_spec=pltpu.PrefetchScalarGridSpec(
            num_scalar_prefetch=1,
            grid=(count * steps,),
            in_specs=[
                pl.BlockSpec((1, rows, depth), lambda j, index: (j // steps, 0, j % steps)),
                pl.BlockSpec((depth, width), lambda j, index: (at(j, index), 0)),
                pl.BlockSpec((1, depth // BLOCK, width), lambda j, index: (at(j, index), 0, 0)),
                pl.BlockSpec((rows, width), lambda j, index: (0, 0)),
            ],
            out_specs=pl.BlockSpec((rows, width), lambda j, index: (0, 0)),
        ),
        out_shape=jax.ShapeDtypeStruct((rows, width), jnp.float32),
        input_output_aliases={4: 0},
        compiler_params=pltpu.CompilerParams(vmem_limit_bytes=32 * 1024 * 1024),
        cost_estimate=pl.CostEstimate(
            flops=2 * rows * width * unit * count,
            bytes_accessed=4 * width * unit * count,
            transcendentals=0,
        ),
        name="down",
    )(index, hidden, w_down, scale, total)


def activate(sums):
    gate, up = sums[0].astype(jnp.float32), sums[1].astype(jnp.float32)
    return (jax.nn.silu(gate) * up).astype(jnp.bfloat16)


def chain_pairs(stages, experts, moving):
    up, back = [], []
    for expert in range(experts):
        for place in moving:
            here, there = place * experts + expert, (place + 1) * experts + expert
            if expert % 2:
                here = (stages - 1 - place) * experts + expert
                there = (stages - 2 - place) * experts + expert
            up.append((here, there))
            back.append((there, here))
    return up, back


def after(value, *done):
    return lax.optimization_barrier((value, *done))[0]


def expert_rows(x, weights, w_down, down_scale):
    stages, experts = lax.axis_size("fsdp"), lax.axis_size("expert")
    hidden_width = weights[0].shape[1]
    unit = hidden_width // UNITS
    chain = CHAIN_UNITS if stages <= 4 else 0
    rest = hidden_width - chain * unit
    rows = x.shape[0]
    total = jnp.zeros((rows, w_down.shape[1]), jnp.float32)

    def call_part():
        index = jnp.array([chain * unit // own_tile(rest), 1], jnp.int32)
        own = own_terms(index, x, weights, rest)
        summed = lax.psum_scatter(own, "fsdp", scatter_dimension=1, tiled=True)
        return lax.all_gather(activate(summed), "fsdp", axis=0, tiled=True)

    def call_down(hidden, total):
        count = UNITS - chain
        stacked = jnp.stack([hidden[:, u * unit : (u + 1) * unit] for u in range(count)])
        index = jnp.array([list(range(chain, UNITS)), [1] * count], jnp.int32)
        return down_add(index, stacked, w_down, down_scale, total)

    if not chain:
        return call_down(call_part(), total)
    line, expert = lax.axis_index("fsdp"), lax.axis_index("expert")
    place = jnp.where(expert % 2 == 0, line, stages - 1 - line)
    last = stages - 1
    reach = LAG * last
    axes = ("fsdp", "expert")

    def own_at(slot, *done):
        held = slot - LAG * place
        counts = (held >= 0) & (held < chain)
        first = jnp.clip(held, 0, chain - 1) * (unit // own_tile(unit))
        index = jnp.stack([first, counts]).astype(jnp.int32)
        return own_terms(after(index, *done) if done else index, x, weights, unit)

    gathered = call_part() if rest else None
    sent, told = {}, {}
    group = []
    own = own_at(0)
    for slot in range(chain + 2 * reach):
        fresh = None
        token = own
        if slot < chain + reach:
            sums = own
            if slot - LAG in sent:
                sums = (
                    sums.astype(jnp.float32) + sent.pop(slot - LAG).astype(jnp.float32)
                ).astype(jnp.bfloat16)
            moving = [p for p in range(last) if 0 <= slot - LAG * p < chain]
            if moving:
                sent[slot] = lax.ppermute(sums, axes, chain_pairs(stages, experts, moving)[0])
            if slot >= reach:
                fresh = activate(sums)
            token = sums
            if slot + 1 < chain + reach:
                own = own_at(slot + 1, sums)
                token = own
        if slot < reach:
            continue
        arrived = told.pop(slot - LAG, None)
        hidden = arrived if fresh is None else fresh
        if fresh is not None and arrived is not None:
            hidden = jnp.where(place == last, after(fresh, token), arrived)
        moving = [p for p in range(last) if 0 <= slot - reach - LAG * (last - 1 - p) < chain]
        if moving:
            told[slot] = lax.ppermute(hidden, axes, chain_pairs(stages, experts, moving)[1])
        held = slot - reach - LAG * (last - place)
        counts = ((held >= 0) & (held < chain)).astype(jnp.int32)
        group.append((jnp.clip(held, 0, chain - 1), counts, hidden))
        if len(group) == GROUP or slot == chain + 2 * reach - 1:
            index = jnp.stack([jnp.stack([g[0] for g in group]), jnp.stack([g[1] for g in group])])
            total = down_add(
                index.astype(jnp.int32), jnp.stack([g[2] for g in group]), w_down, down_scale, total
            )
            group = []
            if slot + 1 < chain + reach:
                own = after(own, total)
            elif slot - LAG + 1 in told:
                told[slot - LAG + 1] = after(told[slot - LAG + 1], total)
    return total if gathered is None else call_down(gathered, total)


def shards(tokens, expert_ids, gate_values, w_gate, w_up, w_down, scale_gate, scale_up, scale_down):
    device_count = lax.axis_size("expert")
    slices = device_count // EXPERTS
    local_tokens = tokens.shape[0]
    feature_cols = tokens.shape[1]
    slot_total = EXPERTS * CAP
    flat_ids = expert_ids.reshape(-1)
    onehot = (flat_ids[:, None] == jnp.arange(EXPERTS, dtype=jnp.int32)[None, :]).astype(jnp.int32)
    slot_rank = jnp.sum((jnp.cumsum(onehot, axis=0) - onehot) * onehot, axis=1)
    target = flat_ids * CAP + slot_rank
    placing = (target[:, None] == jnp.arange(slot_total, dtype=jnp.int32)[None, :]).astype(
        jnp.float32
    )
    token_map = jnp.sum(placing.reshape(local_tokens, 2, slot_total), axis=1).astype(jnp.bfloat16)
    packed = jnp.einsum("ts,td->sd", token_map, tokens, preferred_element_type=jnp.float32).astype(
        jnp.bfloat16
    )
    outgoing = jnp.broadcast_to(
        packed.reshape(EXPERTS, 1, CAP, feature_cols), (EXPERTS, slices, CAP, feature_cols)
    ).reshape(device_count * CAP, feature_cols)
    incoming = lax.all_to_all(outgoing, "expert", split_axis=0, concat_axis=0, tiled=True)
    weights = (w_gate, w_up, widen(scale_gate), widen(scale_up))
    partial_rows = expert_rows(incoming, weights, w_down, widen(scale_down)).astype(jnp.bfloat16)
    returned = lax.all_to_all(partial_rows, "expert", split_axis=0, concat_axis=0, tiled=True)
    slice_sums = jnp.sum(
        returned.reshape(EXPERTS, slices, CAP, feature_cols).astype(jnp.float32), axis=1
    )
    slice_sums = slice_sums.reshape(slot_total, feature_cols)
    weights_map = jnp.sum(
        (placing * gate_values.reshape(-1)[:, None]).reshape(local_tokens, 2, slot_total), axis=1
    )
    mixed_rows = jnp.dot(
        weights_map, slice_sums, precision=lax.Precision.HIGHEST, preferred_element_type=jnp.float32
    )
    return mixed_rows.astype(jnp.bfloat16)


def solution(mesh):
    in_specs = (
        P("expert", "fsdp"),
        P("expert", None),
        P("expert", None),
        P("fsdp", "expert"),
        P("fsdp", "expert"),
        P("expert", "fsdp"),
        P("fsdp", "expert"),
        P("fsdp", "expert"),
        P("expert", "fsdp"),
    )
    out_specs = P("expert", "fsdp")
    return jax.shard_map(shards, mesh=mesh, in_specs=in_specs, out_specs=out_specs, check_vma=False)
```

```python
import functools

import jax
import jax.numpy as jnp
from jax import lax
from jax.experimental import pallas as pl
from jax.experimental.pallas import tpu as pltpu
from jax.sharding import PartitionSpec as P

EXPERTS = 8
BLOCK = 128
CAP = 24
UNITS = 8
CHAIN_UNITS = 8
LAG = 2
HOLD = 2
GROUP = 1


def widen(block_scale):
    return jnp.repeat(block_scale, BLOCK, axis=1).astype(jnp.bfloat16)


def spread(weights, scale_rows):
    depth = weights.shape[0]
    parts = [
        weights[k * BLOCK : (k + 1) * BLOCK, :] * scale_rows[k : k + 1, :]
        for k in range(depth // BLOCK)
    ]
    return jnp.concatenate(parts, axis=0) if len(parts) > 1 else parts[0]


def own_kernel(index_ref, x_ref, gate_ref, up_ref, gate_scale_ref, up_scale_ref, out_ref):
    @pl.when(index_ref[1] > 0)
    def _():
        x = x_ref[...]
        out_ref[0] = jnp.dot(
            x, spread(gate_ref[...], gate_scale_ref[...]), preferred_element_type=jnp.float32
        ).astype(jnp.bfloat16)
        out_ref[1] = jnp.dot(
            x, spread(up_ref[...], up_scale_ref[...]), preferred_element_type=jnp.float32
        ).astype(jnp.bfloat16)


def tile(width, most):
    return max(t for t in range(BLOCK, most + 1, BLOCK) if width % t == 0)


def own_terms(index, x, weights, count):
    w_gate, w_up, gate_scale, up_scale = weights
    rows, depth = x.shape
    width = own_tile(count)
    column = lambda j, index: (0, index[0] + jnp.where(index[1] > 0, j, 0))
    weight_spec = pl.BlockSpec((depth, width), column)
    scale_spec = pl.BlockSpec((depth // BLOCK, width), column)
    return pl.pallas_call(
        own_kernel,
        grid_spec=pltpu.PrefetchScalarGridSpec(
            num_scalar_prefetch=1,
            grid=(count // width,),
            in_specs=[
                pl.BlockSpec((rows, depth), lambda j, index: (0, 0)),
                weight_spec,
                weight_spec,
                scale_spec,
                scale_spec,
            ],
            out_specs=pl.BlockSpec((2, rows, width), lambda j, index: (0, 0, j)),
        ),
        out_shape=jax.ShapeDtypeStruct((2, rows, count), jnp.bfloat16),
        compiler_params=pltpu.CompilerParams(vmem_limit_bytes=32 * 1024 * 1024),
        cost_estimate=pl.CostEstimate(
            flops=rows * depth * count // 8, bytes_accessed=depth * count // 8, transcendentals=0
        ),
        name="gate_up",
    )(index, x, w_gate, w_up, gate_scale, up_scale)


def own_tile(count):
    return tile(count, 512)


def down_kernel(index_ref, hidden_ref, weight_ref, scale_ref, total_ref, out_ref, *, steps):
    step = pl.program_id(0)

    @pl.when(step == 0)
    def _():
        out_ref[...] = total_ref[...]

    @pl.when(index_ref[1, step // steps] > 0)
    def _():
        out_ref[...] += jnp.dot(
            hidden_ref[0],
            spread(weight_ref[...], scale_ref[0]),
            preferred_element_type=jnp.float32,
        )


def down_add(index, hidden, w_down, down_scale, total):
    count, rows, unit = hidden.shape
    width = w_down.shape[1]
    depth = tile(unit, 512)
    steps = unit // depth

    def at(j, index):
        slot = j // steps
        return index[0, slot] * steps + jnp.where(index[1, slot] > 0, j % steps, 0)

    scale = down_scale.reshape(-1, depth // BLOCK, width)
    return pl.pallas_call(
        functools.partial(down_kernel, steps=steps),
        grid_spec=pltpu.PrefetchScalarGridSpec(
            num_scalar_prefetch=1,
            grid=(count * steps,),
            in_specs=[
                pl.BlockSpec((1, rows, depth), lambda j, index: (j // steps, 0, j % steps)),
                pl.BlockSpec((depth, width), lambda j, index: (at(j, index), 0)),
                pl.BlockSpec((1, depth // BLOCK, width), lambda j, index: (at(j, index), 0, 0)),
                pl.BlockSpec((rows, width), lambda j, index: (0, 0)),
            ],
            out_specs=pl.BlockSpec((rows, width), lambda j, index: (0, 0)),
        ),
        out_shape=jax.ShapeDtypeStruct((rows, width), jnp.float32),
        input_output_aliases={4: 0},
        compiler_params=pltpu.CompilerParams(vmem_limit_bytes=32 * 1024 * 1024),
        cost_estimate=pl.CostEstimate(
            flops=rows * width * unit * count // 16,
            bytes_accessed=width * unit * count // 16,
            transcendentals=0,
        ),
        name="down",
    )(index, hidden, w_down, scale, total)


def activate(sums):
    gate, up = sums[0].astype(jnp.float32), sums[1].astype(jnp.float32)
    return (jax.nn.silu(gate) * up).astype(jnp.bfloat16)


def chain_pairs(stages, experts, moving):
    up, back = [], []
    for expert in range(experts):
        for place in moving:
            here, there = place * experts + expert, (place + 1) * experts + expert
            if expert % 2:
                here = (stages - 1 - place) * experts + expert
                there = (stages - 2 - place) * experts + expert
            up.append((here, there))
            back.append((there, here))
    return up, back


def after(value, *done):
    return lax.optimization_barrier((value, *done))[0]


def expert_rows(x, weights, w_down, down_scale):
    stages, experts = lax.axis_size("fsdp"), lax.axis_size("expert")
    hidden_width = weights[0].shape[1]
    unit = hidden_width // UNITS
    chain = CHAIN_UNITS if stages <= 4 else 0
    rest = hidden_width - chain * unit
    rows = x.shape[0]
    total = jnp.zeros((rows, w_down.shape[1]), jnp.float32)

    def call_part():
        index = jnp.array([chain * unit // own_tile(rest), 1], jnp.int32)
        own = own_terms(index, x, weights, rest)
        summed = lax.psum_scatter(own, "fsdp", scatter_dimension=1, tiled=True)
        return lax.all_gather(activate(summed), "fsdp", axis=0, tiled=True)

    def call_down(hidden, total):
        count = UNITS - chain
        stacked = jnp.stack([hidden[:, u * unit : (u + 1) * unit] for u in range(count)])
        index = jnp.array([list(range(chain, UNITS)), [1] * count], jnp.int32)
        return down_add(index, stacked, w_down, down_scale, total)

    if not chain:
        return call_down(call_part(), total)
    line, expert = lax.axis_index("fsdp"), lax.axis_index("expert")
    place = jnp.where(expert % 2 == 0, line, stages - 1 - line)
    last = stages - 1
    reach = LAG * last
    axes = ("fsdp", "expert")

    def own_at(slot, *done):
        held = slot - LAG * place
        counts = (held >= 0) & (held < chain)
        first = jnp.clip(held, 0, chain - 1) * (unit // own_tile(unit))
        index = jnp.stack([first, counts]).astype(jnp.int32)
        return own_terms(after(index, *done) if done else index, x, weights, unit)

    def hidden_of(number):
        chosen = None
        for p in range(stages):
            value = held[number + begin + LAG * (last - p)]
            chosen = value if chosen is None else jnp.where(place == p, value, chosen)
        return chosen

    gathered = call_part() if rest else None
    begin = reach + HOLD
    sent, fresh, held, told = {}, {}, {}, {}
    own = own_at(0)
    token = own
    finished = 0
    for slot in range(chain + begin + reach):
        if slot < chain + reach:
            sums = own
            if slot - LAG in sent:
                arrived = after(sent.pop(slot - LAG), token)
                sums = (sums.astype(jnp.float32) + arrived.astype(jnp.float32)).astype(jnp.bfloat16)
            moving = [p for p in range(last) if 0 <= slot - LAG * p < chain]
            if moving:
                sent[slot] = lax.ppermute(sums, axes, chain_pairs(stages, experts, moving)[0])
            token = sums
            if slot >= reach:
                fresh[slot + HOLD] = activate(sums)
                token = fresh[slot + HOLD]
            if slot + 1 < chain + reach:
                own = own_at(slot + 1, token)
                token = own
        if slot < begin:
            continue
        hidden = fresh.get(slot)
        if slot - LAG in told:
            arrived = after(told.pop(slot - LAG), token)
            hidden = arrived if hidden is None else jnp.where(place == last, hidden, arrived)
        moving = [p for p in range(last) if 0 <= slot - begin - LAG * (last - 1 - p) < chain]
        if moving:
            told[slot] = lax.ppermute(hidden, axes, chain_pairs(stages, experts, moving)[1])
        held[slot] = hidden
        token = hidden
        complete = slot + 1 - begin - reach
        if complete - finished >= GROUP or complete == chain:
            units = list(range(finished, complete))
            stacked = jnp.stack([hidden_of(u) for u in units])
            index = jnp.array([units, [1] * len(units)], jnp.int32)
            total = down_add(after(index, token), stacked, w_down, down_scale, total)
            finished = complete
            token = total
    return total if gathered is None else call_down(gathered, total)


def shards(tokens, expert_ids, gate_values, w_gate, w_up, w_down, scale_gate, scale_up, scale_down):
    device_count = lax.axis_size("expert")
    slices = device_count // EXPERTS
    local_tokens = tokens.shape[0]
    feature_cols = tokens.shape[1]
    slot_total = EXPERTS * CAP
    flat_ids = expert_ids.reshape(-1)
    onehot = (flat_ids[:, None] == jnp.arange(EXPERTS, dtype=jnp.int32)[None, :]).astype(jnp.int32)
    slot_rank = jnp.sum((jnp.cumsum(onehot, axis=0) - onehot) * onehot, axis=1)
    target = flat_ids * CAP + slot_rank
    placing = (target[:, None] == jnp.arange(slot_total, dtype=jnp.int32)[None, :]).astype(
        jnp.float32
    )
    token_map = jnp.sum(placing.reshape(local_tokens, 2, slot_total), axis=1).astype(jnp.bfloat16)
    packed = jnp.einsum("ts,td->sd", token_map, tokens, preferred_element_type=jnp.float32).astype(
        jnp.bfloat16
    )
    outgoing = jnp.broadcast_to(
        packed.reshape(EXPERTS, 1, CAP, feature_cols), (EXPERTS, slices, CAP, feature_cols)
    ).reshape(device_count * CAP, feature_cols)
    incoming = lax.all_to_all(outgoing, "expert", split_axis=0, concat_axis=0, tiled=True)
    weights = (w_gate, w_up, widen(scale_gate), widen(scale_up))
    partial_rows = expert_rows(incoming, weights, w_down, widen(scale_down)).astype(jnp.bfloat16)
    returned = lax.all_to_all(partial_rows, "expert", split_axis=0, concat_axis=0, tiled=True)
    slice_sums = jnp.sum(
        returned.reshape(EXPERTS, slices, CAP, feature_cols).astype(jnp.float32), axis=1
    )
    slice_sums = slice_sums.reshape(slot_total, feature_cols)
    weights_map = jnp.sum(
        (placing * gate_values.reshape(-1)[:, None]).reshape(local_tokens, 2, slot_total), axis=1
    )
    mixed_rows = jnp.dot(
        weights_map, slice_sums, precision=lax.Precision.HIGHEST, preferred_element_type=jnp.float32
    )
    return mixed_rows.astype(jnp.bfloat16)


def solution(mesh):
    in_specs = (
        P("expert", "fsdp"),
        P("expert", None),
        P("expert", None),
        P("fsdp", "expert"),
        P("fsdp", "expert"),
        P("expert", "fsdp"),
        P("fsdp", "expert"),
        P("fsdp", "expert"),
        P("expert", "fsdp"),
    )
    out_specs = P("expert", "fsdp")
    return jax.shard_map(shards, mesh=mesh, in_specs=in_specs, out_specs=out_specs, check_vma=False)
```

```python
import functools

import jax
import jax.numpy as jnp
from jax import lax
from jax.experimental import pallas as pl
from jax.experimental.pallas import tpu as pltpu
from jax.sharding import PartitionSpec as P

EXPERTS = 8
BLOCK = 128
CAP = 24
UNITS = 8
CHAIN_UNITS = 8
LAG = 2
HOLD = 2
GROUP = 1


def widen(block_scale):
    return jnp.repeat(block_scale, BLOCK, axis=1).astype(jnp.bfloat16)


def spread(weights, scale_rows):
    depth = weights.shape[0]
    parts = [
        weights[k * BLOCK : (k + 1) * BLOCK, :] * scale_rows[k : k + 1, :]
        for k in range(depth // BLOCK)
    ]
    return jnp.concatenate(parts, axis=0) if len(parts) > 1 else parts[0]


def own_kernel(index_ref, x_ref, gate_ref, up_ref, gate_scale_ref, up_scale_ref, out_ref):
    @pl.when(index_ref[1] > 0)
    def _():
        x = x_ref[...]
        out_ref[0] = jnp.dot(
            x, spread(gate_ref[...], gate_scale_ref[...]), preferred_element_type=jnp.float32
        ).astype(jnp.bfloat16)
        out_ref[1] = jnp.dot(
            x, spread(up_ref[...], up_scale_ref[...]), preferred_element_type=jnp.float32
        ).astype(jnp.bfloat16)


def tile(width, most):
    return max(t for t in range(BLOCK, most + 1, BLOCK) if width % t == 0)


def own_terms(index, x, weights, count):
    w_gate, w_up, gate_scale, up_scale = weights
    rows, depth = x.shape
    width = own_tile(count)
    column = lambda j, index: (0, index[0] + jnp.where(index[1] > 0, j, 0))
    weight_spec = pl.BlockSpec((depth, width), column)
    scale_spec = pl.BlockSpec((depth // BLOCK, width), column)
    return pl.pallas_call(
        own_kernel,
        grid_spec=pltpu.PrefetchScalarGridSpec(
            num_scalar_prefetch=1,
            grid=(count // width,),
            in_specs=[
                pl.BlockSpec((rows, depth), lambda j, index: (0, 0)),
                weight_spec,
                weight_spec,
                scale_spec,
                scale_spec,
            ],
            out_specs=pl.BlockSpec((2, rows, width), lambda j, index: (0, 0, j)),
        ),
        out_shape=jax.ShapeDtypeStruct((2, rows, count), jnp.bfloat16),
        compiler_params=pltpu.CompilerParams(vmem_limit_bytes=32 * 1024 * 1024),
        cost_estimate=pl.CostEstimate(
            flops=rows * depth * count // 8, bytes_accessed=depth * count // 8, transcendentals=0
        ),
        name="gate_up",
    )(index, x, w_gate, w_up, gate_scale, up_scale)


def own_tile(count):
    return tile(count, 512)


def down_kernel(index_ref, hidden_ref, weight_ref, scale_ref, total_ref, out_ref, *, steps):
    step = pl.program_id(0)

    @pl.when(step == 0)
    def _():
        out_ref[...] = total_ref[...]

    @pl.when(index_ref[1, step // steps] > 0)
    def _():
        out_ref[...] += jnp.dot(
            hidden_ref[0],
            spread(weight_ref[...], scale_ref[0]),
            preferred_element_type=jnp.float32,
        )


def down_add(index, hidden, w_down, down_scale, total):
    count, rows, unit = hidden.shape
    width = w_down.shape[1]
    depth = tile(unit, 512)
    steps = unit // depth

    def at(j, index):
        slot = j // steps
        return index[0, slot] * steps + jnp.where(index[1, slot] > 0, j % steps, 0)

    scale = down_scale.reshape(-1, depth // BLOCK, width)
    return pl.pallas_call(
        functools.partial(down_kernel, steps=steps),
        grid_spec=pltpu.PrefetchScalarGridSpec(
            num_scalar_prefetch=1,
            grid=(count * steps,),
            in_specs=[
                pl.BlockSpec((1, rows, depth), lambda j, index: (j // steps, 0, j % steps)),
                pl.BlockSpec((depth, width), lambda j, index: (at(j, index), 0)),
                pl.BlockSpec((1, depth // BLOCK, width), lambda j, index: (at(j, index), 0, 0)),
                pl.BlockSpec((rows, width), lambda j, index: (0, 0)),
            ],
            out_specs=pl.BlockSpec((rows, width), lambda j, index: (0, 0)),
        ),
        out_shape=jax.ShapeDtypeStruct((rows, width), jnp.float32),
        input_output_aliases={4: 0},
        compiler_params=pltpu.CompilerParams(vmem_limit_bytes=32 * 1024 * 1024),
        cost_estimate=pl.CostEstimate(
            flops=rows * width * unit * count // 16,
            bytes_accessed=width * unit * count // 16,
            transcendentals=0,
        ),
        name="down",
    )(index, hidden, w_down, scale, total)


def activate(sums):
    gate, up = sums[0].astype(jnp.float32), sums[1].astype(jnp.float32)
    return (jax.nn.silu(gate) * up).astype(jnp.bfloat16)


def chain_pairs(stages, experts, moving):
    up, back = [], []
    for expert in range(experts):
        for place in moving:
            here, there = place * experts + expert, (place + 1) * experts + expert
            if expert % 2:
                here = (stages - 1 - place) * experts + expert
                there = (stages - 2 - place) * experts + expert
            up.append((here, there))
            back.append((there, here))
    return up, back


def after(value, *done):
    return lax.optimization_barrier((value, *done))[0]


def expert_rows(x, weights, w_down, down_scale):
    stages, experts = lax.axis_size("fsdp"), lax.axis_size("expert")
    hidden_width = weights[0].shape[1]
    unit = hidden_width // UNITS
    chain = CHAIN_UNITS if stages <= 4 else 0
    rest = hidden_width - chain * unit
    rows = x.shape[0]
    total = jnp.zeros((rows, w_down.shape[1]), jnp.float32)

    def call_part():
        index = jnp.array([chain * unit // own_tile(rest), 1], jnp.int32)
        own = own_terms(index, x, weights, rest)
        summed = lax.psum_scatter(own, "fsdp", scatter_dimension=1, tiled=True)
        return lax.all_gather(activate(summed), "fsdp", axis=0, tiled=True)

    def call_down(hidden, total):
        count = UNITS - chain
        stacked = jnp.stack([hidden[:, u * unit : (u + 1) * unit] for u in range(count)])
        index = jnp.array([list(range(chain, UNITS)), [1] * count], jnp.int32)
        return down_add(index, stacked, w_down, down_scale, total)

    if not chain:
        return call_down(call_part(), total)
    line, expert = lax.axis_index("fsdp"), lax.axis_index("expert")
    place = jnp.where(expert % 2 == 0, line, stages - 1 - line)
    last = stages - 1
    reach = LAG * last
    axes = ("fsdp", "expert")

    def own_at(slot, *done):
        held = slot - LAG * place
        counts = (held >= 0) & (held < chain)
        first = jnp.clip(held, 0, chain - 1) * (unit // own_tile(unit))
        index = jnp.stack([first, counts]).astype(jnp.int32)
        return own_terms(after(index, *done) if done else index, x, weights, unit)

    def hidden_of(number):
        chosen = None
        for p in range(stages):
            value = held[number + begin + LAG * (last - p)]
            chosen = value if chosen is None else jnp.where(place == p, value, chosen)
        return chosen

    gathered = call_part() if rest else None
    begin = reach + HOLD
    sent, fresh, held, told = {}, {}, {}, {}
    own = own_at(0)
    token = own
    finished = 0
    for slot in range(chain + begin + reach):
        if slot < chain + reach:
            sums = own
            if slot - LAG in sent:
                arrived = after(sent.pop(slot - LAG), token)
                sums = (sums.astype(jnp.float32) + arrived.astype(jnp.float32)).astype(jnp.bfloat16)
            moving = [p for p in range(last) if 0 <= slot - LAG * p < chain]
            if moving:
                sent[slot] = lax.ppermute(sums, axes, chain_pairs(stages, experts, moving)[0])
            token = sums
            if slot >= reach:
                fresh[slot + HOLD] = activate(sums)
                token = fresh[slot + HOLD]
        if slot < begin:
            own = own_at(slot + 1, token)
            token = own
            continue
        hidden = fresh.get(slot)
        if slot - LAG in told:
            arrived = after(told.pop(slot - LAG), token)
            hidden = arrived if hidden is None else jnp.where(place == last, hidden, arrived)
        moving = [p for p in range(last) if 0 <= slot - begin - LAG * (last - 1 - p) < chain]
        if moving:
            told[slot] = lax.ppermute(hidden, axes, chain_pairs(stages, experts, moving)[1])
        held[slot] = hidden
        token = hidden
        if slot + 1 < chain + reach:
            own = own_at(slot + 1, token)
            token = own
        complete = slot + 1 - begin - reach
        if complete - finished >= GROUP or complete == chain:
            units = list(range(finished, complete))
            stacked = jnp.stack([hidden_of(u) for u in units])
            index = jnp.array([units, [1] * len(units)], jnp.int32)
            total = down_add(after(index, token), stacked, w_down, down_scale, total)
            finished = complete
            token = total
    return total if gathered is None else call_down(gathered, total)


def shards(tokens, expert_ids, gate_values, w_gate, w_up, w_down, scale_gate, scale_up, scale_down):
    device_count = lax.axis_size("expert")
    slices = device_count // EXPERTS
    local_tokens = tokens.shape[0]
    feature_cols = tokens.shape[1]
    slot_total = EXPERTS * CAP
    flat_ids = expert_ids.reshape(-1)
    onehot = (flat_ids[:, None] == jnp.arange(EXPERTS, dtype=jnp.int32)[None, :]).astype(jnp.int32)
    slot_rank = jnp.sum((jnp.cumsum(onehot, axis=0) - onehot) * onehot, axis=1)
    target = flat_ids * CAP + slot_rank
    placing = (target[:, None] == jnp.arange(slot_total, dtype=jnp.int32)[None, :]).astype(
        jnp.float32
    )
    token_map = jnp.sum(placing.reshape(local_tokens, 2, slot_total), axis=1).astype(jnp.bfloat16)
    packed = jnp.einsum("ts,td->sd", token_map, tokens, preferred_element_type=jnp.float32).astype(
        jnp.bfloat16
    )
    outgoing = jnp.broadcast_to(
        packed.reshape(EXPERTS, 1, CAP, feature_cols), (EXPERTS, slices, CAP, feature_cols)
    ).reshape(device_count * CAP, feature_cols)
    incoming = lax.all_to_all(outgoing, "expert", split_axis=0, concat_axis=0, tiled=True)
    weights = (w_gate, w_up, widen(scale_gate), widen(scale_up))
    partial_rows = expert_rows(incoming, weights, w_down, widen(scale_down)).astype(jnp.bfloat16)
    returned = lax.all_to_all(partial_rows, "expert", split_axis=0, concat_axis=0, tiled=True)
    slice_sums = jnp.sum(
        returned.reshape(EXPERTS, slices, CAP, feature_cols).astype(jnp.float32), axis=1
    )
    slice_sums = slice_sums.reshape(slot_total, feature_cols)
    weights_map = jnp.sum(
        (placing * gate_values.reshape(-1)[:, None]).reshape(local_tokens, 2, slot_total), axis=1
    )
    mixed_rows = jnp.dot(
        weights_map, slice_sums, precision=lax.Precision.HIGHEST, preferred_element_type=jnp.float32
    )
    return mixed_rows.astype(jnp.bfloat16)


def solution(mesh):
    in_specs = (
        P("expert", "fsdp"),
        P("expert", None),
        P("expert", None),
        P("fsdp", "expert"),
        P("fsdp", "expert"),
        P("expert", "fsdp"),
        P("fsdp", "expert"),
        P("fsdp", "expert"),
        P("expert", "fsdp"),
    )
    out_specs = P("expert", "fsdp")
    return jax.shard_map(shards, mesh=mesh, in_specs=in_specs, out_specs=out_specs, check_vma=False)
```

```python
import functools

import jax
import jax.numpy as jnp
from jax import lax
from jax.experimental import pallas as pl
from jax.experimental.pallas import tpu as pltpu
from jax.sharding import PartitionSpec as P

EXPERTS = 8
BLOCK = 128
CAP = 24
UNITS = 8
CHAIN_UNITS = 8
LAG = 2
HOLD = 2
GROUP = 1


def widen(block_scale):
    return jnp.repeat(block_scale, BLOCK, axis=1).astype(jnp.bfloat16)


def spread(weights, scale_rows):
    depth = weights.shape[0]
    parts = [
        weights[k * BLOCK : (k + 1) * BLOCK, :] * scale_rows[k : k + 1, :]
        for k in range(depth // BLOCK)
    ]
    return jnp.concatenate(parts, axis=0) if len(parts) > 1 else parts[0]


def own_kernel(index_ref, x_ref, gate_ref, up_ref, gate_scale_ref, up_scale_ref, out_ref):
    @pl.when(index_ref[1] > 0)
    def _():
        x = x_ref[...]
        out_ref[0] = jnp.dot(
            x, spread(gate_ref[...], gate_scale_ref[...]), preferred_element_type=jnp.float32
        ).astype(jnp.bfloat16)
        out_ref[1] = jnp.dot(
            x, spread(up_ref[...], up_scale_ref[...]), preferred_element_type=jnp.float32
        ).astype(jnp.bfloat16)


def tile(width, most):
    return max(t for t in range(BLOCK, most + 1, BLOCK) if width % t == 0)


def own_terms(index, x, weights, count):
    w_gate, w_up, gate_scale, up_scale = weights
    rows, depth = x.shape
    width = own_tile(count)
    column = lambda j, index: (0, index[0] + jnp.where(index[1] > 0, j, 0))
    weight_spec = pl.BlockSpec((depth, width), column)
    scale_spec = pl.BlockSpec((depth // BLOCK, width), column)
    return pl.pallas_call(
        own_kernel,
        grid_spec=pltpu.PrefetchScalarGridSpec(
            num_scalar_prefetch=1,
            grid=(count // width,),
            in_specs=[
                pl.BlockSpec((rows, depth), lambda j, index: (0, 0)),
                weight_spec,
                weight_spec,
                scale_spec,
                scale_spec,
            ],
            out_specs=pl.BlockSpec((2, rows, width), lambda j, index: (0, 0, j)),
        ),
        out_shape=jax.ShapeDtypeStruct((2, rows, count), jnp.bfloat16),
        compiler_params=pltpu.CompilerParams(vmem_limit_bytes=32 * 1024 * 1024),
        cost_estimate=pl.CostEstimate(
            flops=rows * depth * count // 8, bytes_accessed=depth * count // 8, transcendentals=0
        ),
        name="gate_up",
    )(index, x, w_gate, w_up, gate_scale, up_scale)


def own_tile(count):
    return tile(count, 512)


def down_kernel(index_ref, hidden_ref, weight_ref, scale_ref, total_ref, out_ref, *, steps):
    step = pl.program_id(0)

    @pl.when(step == 0)
    def _():
        out_ref[...] = total_ref[...]

    @pl.when(index_ref[1, step // steps] > 0)
    def _():
        out_ref[...] += jnp.dot(
            hidden_ref[0],
            spread(weight_ref[...], scale_ref[0]),
            preferred_element_type=jnp.float32,
        )


def down_add(index, hidden, w_down, down_scale, total):
    count, rows, unit = hidden.shape
    width = w_down.shape[1]
    depth = tile(unit, 512)
    steps = unit // depth

    def at(j, index):
        slot = j // steps
        return index[0, slot] * steps + jnp.where(index[1, slot] > 0, j % steps, 0)

    scale = down_scale.reshape(-1, depth // BLOCK, width)
    return pl.pallas_call(
        functools.partial(down_kernel, steps=steps),
        grid_spec=pltpu.PrefetchScalarGridSpec(
            num_scalar_prefetch=1,
            grid=(count * steps,),
            in_specs=[
                pl.BlockSpec((1, rows, depth), lambda j, index: (j // steps, 0, j % steps)),
                pl.BlockSpec((depth, width), lambda j, index: (at(j, index), 0)),
                pl.BlockSpec((1, depth // BLOCK, width), lambda j, index: (at(j, index), 0, 0)),
                pl.BlockSpec((rows, width), lambda j, index: (0, 0)),
            ],
            out_specs=pl.BlockSpec((rows, width), lambda j, index: (0, 0)),
        ),
        out_shape=jax.ShapeDtypeStruct((rows, width), jnp.float32),
        input_output_aliases={4: 0},
        compiler_params=pltpu.CompilerParams(vmem_limit_bytes=32 * 1024 * 1024),
        cost_estimate=pl.CostEstimate(
            flops=rows * width * unit * count // 16,
            bytes_accessed=width * unit * count // 16,
            transcendentals=0,
        ),
        name="down",
    )(index, hidden, w_down, scale, total)


def activate(sums):
    gate, up = sums[0].astype(jnp.float32), sums[1].astype(jnp.float32)
    return (jax.nn.silu(gate) * up).astype(jnp.bfloat16)


def chain_pairs(stages, experts, moving):
    up, back = [], []
    for expert in range(experts):
        for place in moving:
            here, there = place * experts + expert, (place + 1) * experts + expert
            if expert % 2:
                here = (stages - 1 - place) * experts + expert
                there = (stages - 2 - place) * experts + expert
            up.append((here, there))
            back.append((there, here))
    return up, back


def after(value, *done):
    return lax.optimization_barrier((value, *done))[0]


def expert_rows(x, weights, w_down, down_scale):
    stages, experts = lax.axis_size("fsdp"), lax.axis_size("expert")
    hidden_width = weights[0].shape[1]
    unit = hidden_width // UNITS
    chain = CHAIN_UNITS if stages <= 4 else 0
    rest = hidden_width - chain * unit
    rows = x.shape[0]
    total = jnp.zeros((rows, w_down.shape[1]), jnp.float32)

    def call_part():
        index = jnp.array([chain * unit // own_tile(rest), 1], jnp.int32)
        own = own_terms(index, x, weights, rest)
        summed = lax.psum_scatter(own, "fsdp", scatter_dimension=1, tiled=True)
        return lax.all_gather(activate(summed), "fsdp", axis=0, tiled=True)

    def call_down(hidden, total):
        count = UNITS - chain
        stacked = jnp.stack([hidden[:, u * unit : (u + 1) * unit] for u in range(count)])
        index = jnp.array([list(range(chain, UNITS)), [1] * count], jnp.int32)
        return down_add(index, stacked, w_down, down_scale, total)

    if not chain:
        return call_down(call_part(), total)
    line, expert = lax.axis_index("fsdp"), lax.axis_index("expert")
    place = jnp.where(expert % 2 == 0, line, stages - 1 - line)
    last = stages - 1
    reach = LAG * last
    axes = ("fsdp", "expert")

    def own_at(slot, *done):
        held = slot - LAG * place
        counts = (held >= 0) & (held < chain)
        first = jnp.clip(held, 0, chain - 1) * (unit // own_tile(unit))
        index = jnp.stack([first, counts]).astype(jnp.int32)
        return own_terms(after(index, *done) if done else index, x, weights, unit)

    def hidden_of(number):
        chosen = None
        for p in range(stages):
            value = held[number + begin + LAG * (last - p)]
            chosen = value if chosen is None else jnp.where(place == p, value, chosen)
        return chosen

    gathered = call_part() if rest else None
    begin = reach + HOLD
    sent, fresh, held, told = {}, {}, {}, {}
    own = own_at(0)
    token = own
    finished = 0
    for slot in range(chain + begin + reach):
        if slot < chain + reach:
            sums = own
            if slot - LAG in sent:
                arrived = after(sent.pop(slot - LAG), token)
                sums = (sums.astype(jnp.float32) + arrived.astype(jnp.float32)).astype(jnp.bfloat16)
            moving = [p for p in range(last) if 0 <= slot - LAG * p < chain]
            if moving:
                sent[slot] = lax.ppermute(sums, axes, chain_pairs(stages, experts, moving)[0])
            token = sums
            if slot >= reach:
                fresh[slot + HOLD] = activate(sums)
                token = fresh[slot + HOLD]
        if slot < begin:
            own = own_at(slot + 1, token)
            token = own
            continue
        hidden = fresh.get(slot)
        if slot - LAG in told:
            arrived = after(told.pop(slot - LAG), token)
            hidden = arrived if hidden is None else jnp.where(place == last, hidden, arrived)
        moving = [p for p in range(last) if 0 <= slot - begin - LAG * (last - 1 - p) < chain]
        if moving:
            told[slot] = lax.ppermute(hidden, axes, chain_pairs(stages, experts, moving)[1])
        held[slot] = hidden
        token = hidden
        if slot + 1 < chain + reach:
            own = own_at(slot + 1, token)
            token = own
        complete = slot + 1 - begin - reach
        if complete - finished >= GROUP or complete == chain:
            units = list(range(finished, complete))
            stacked = jnp.stack([hidden_of(u) for u in units])
            index = jnp.array([units, [1] * len(units)], jnp.int32)
            total = down_add(after(index, token), stacked, w_down, down_scale, total)
            finished = complete
            token = total
    return total if gathered is None else call_down(gathered, total)


def shards(tokens, expert_ids, gate_values, w_gate, w_up, w_down, scale_gate, scale_up, scale_down):
    device_count = lax.axis_size("expert")
    slices = device_count // EXPERTS
    local_tokens = tokens.shape[0]
    feature_cols = tokens.shape[1]
    slot_total = EXPERTS * CAP
    flat_ids = expert_ids.reshape(-1)
    onehot = (flat_ids[:, None] == jnp.arange(EXPERTS, dtype=jnp.int32)[None, :]).astype(jnp.int32)
    slot_rank = jnp.sum((jnp.cumsum(onehot, axis=0) - onehot) * onehot, axis=1)
    target = flat_ids * CAP + slot_rank
    placing = (target[:, None] == jnp.arange(slot_total, dtype=jnp.int32)[None, :]).astype(
        jnp.float32
    )
    numbers = jnp.arange(EXPERTS, dtype=jnp.int32)[None, :]
    chosen = [(expert_ids[:, k : k + 1] == numbers).astype(jnp.int32) for k in range(2)]
    prior = jnp.cumsum(chosen[0] + chosen[1], axis=0) - chosen[0] - chosen[1]
    first, second = [
        expert_ids[:, k : k + 1] * CAP + jnp.sum(prior * chosen[k], axis=1, keepdims=True)
        == jnp.arange(slot_total, dtype=jnp.int32)[None, :]
        for k in range(2)
    ]
    token_map = (first | second).astype(jnp.bfloat16)
    packed = jnp.einsum("ts,td->sd", token_map, tokens, preferred_element_type=jnp.float32).astype(
        jnp.bfloat16
    )
    outgoing = jnp.broadcast_to(
        packed.reshape(EXPERTS, 1, CAP, feature_cols), (EXPERTS, slices, CAP, feature_cols)
    ).reshape(device_count * CAP, feature_cols)
    incoming = lax.all_to_all(outgoing, "expert", split_axis=0, concat_axis=0, tiled=True)
    weights = (w_gate, w_up, widen(scale_gate), widen(scale_up))
    partial_rows = expert_rows(incoming, weights, w_down, widen(scale_down)).astype(jnp.bfloat16)
    returned = lax.all_to_all(partial_rows, "expert", split_axis=0, concat_axis=0, tiled=True)
    slice_sums = jnp.sum(
        returned.reshape(EXPERTS, slices, CAP, feature_cols).astype(jnp.float32), axis=1
    )
    slice_sums = slice_sums.reshape(slot_total, feature_cols)
    weights_map = jnp.sum(
        (placing * gate_values.reshape(-1)[:, None]).reshape(local_tokens, 2, slot_total), axis=1
    )
    mixed_rows = jnp.dot(
        weights_map, slice_sums, precision=lax.Precision.HIGHEST, preferred_element_type=jnp.float32
    )
    return mixed_rows.astype(jnp.bfloat16)


def solution(mesh):
    in_specs = (
        P("expert", "fsdp"),
        P("expert", None),
        P("expert", None),
        P("fsdp", "expert"),
        P("fsdp", "expert"),
        P("expert", "fsdp"),
        P("fsdp", "expert"),
        P("fsdp", "expert"),
        P("expert", "fsdp"),
    )
    out_specs = P("expert", "fsdp")
    return jax.shard_map(shards, mesh=mesh, in_specs=in_specs, out_specs=out_specs, check_vma=False)
```
